32 devices in a mesh: tmpl: 8 (over z, y), tm: 4 (over x, core).
Axes of the slice: x: 2, y: 2, z: 4, core: 2. Of those that a mesh axis runs over, the one named last changes fastest.
Arguments:
- records: bfloat16 [8, 64, 2048], P('tmpl', None, 'tm'), may hold values from -80 to 80
- templates: bfloat16 [16, 64, 256], P('tmpl'), may hold values from -6 to 6
Outputs:
- detection: float32 [8, 16, 2048], P(None, 'tmpl', 'tm')
The draws below stay inside these ranges and needn't reach their ends.
All inputs are finite; a program needn't handle non-finite values.
Results may differ from the reference program's by a relative error of at most 0.0041.
Values may be sent and summed in bfloat16 or wider, within the bound.
A program may use at most 64 MiB of HBM per device.

```python
import math
import jax
import jax.numpy as jnp
from jax import lax

C = 64
L = 256
TEMPLATES = 16
WINDOWS = 8
S = 2048


def draw_records(key, part):
    first, second, third = jax.random.split(key, 3)
    base = jax.random.truncated_normal(first, -4.0, 4.0, (WINDOWS, C, S), jnp.float32)
    channel_gain = jnp.exp(jax.random.uniform(second, (WINDOWS, C, 1), jnp.float32, 0.0, math.log(10.0)))
    envelope = jnp.exp(jax.random.uniform(third, (WINDOWS, C, S // 16, 1), jnp.float32, math.log(0.5), math.log(2.0)))
    envelope = jnp.broadcast_to(envelope, (WINDOWS, C, S // 16, 16)).reshape(WINDOWS, C, S)
    return (base * channel_gain * envelope).astype(jnp.bfloat16)


def block_levels(own_key, dims, cuts, low, top_value):
    factor_of = 1.0
    for dim, shards_of in cuts:
        steps = jax.random.uniform(jax.random.fold_in(jax.random.fold_in(own_key, 6), dim), (shards_of,), jnp.float32, low / len(cuts), top_value / len(cuts))
        factor_of = factor_of * jnp.repeat(jnp.exp(steps), dims[dim] // shards_of).reshape((-1,) + (1,) * (len(dims) - 1 - dim))
    return factor_of


def noise(rng, dims, deviation, limit, cuts=(), held_as=jnp.bfloat16):
    drawn = jax.random.normal(rng, dims, jnp.float32) * deviation
    if len(cuts) > 0:
        drawn = block_levels(rng, dims, cuts, -0.22, 0.18) * drawn
    return jnp.clip(drawn, min=-limit, max=limit).astype(held_as)


def setup_inputs(seed: int = 0) -> dict:
    splits = jax.random.split(jax.random.key(seed), 3)
    return {
        "records": draw_records(jax.random.fold_in(splits[2], 71), 0),
        "templates": noise(splits[1], (TEMPLATES, C, L), 1.0, 6.0, ((0, 8),)),
    }


def make_weighted(block):
    wide = block.astype(jnp.float32)
    tinv = lax.rsqrt(lax.optimization_barrier(jnp.sum(wide * wide, axis=2)) + 1e-06)
    weighted = (wide * tinv[:, :, None]).astype(jnp.bfloat16)
    return weighted.reshape(block.shape[0], block.shape[1] * block.shape[2])

def sliding_scale(extended, length):
    count_w, chans, total = extended.shape
    out_len = total - length + 1
    wide = extended.astype(jnp.float32)
    squares = wide * wide
    squares = jnp.concatenate([squares, jnp.zeros((count_w, chans, 1), jnp.float32)], axis=2)
    nblocks = (out_len + length) // 16
    blocks = squares.reshape(count_w, chans, nblocks, 16)
    block_sum = lax.optimization_barrier(jnp.sum(blocks, axis=3))
    prefix = jnp.cumsum(blocks, axis=3) - blocks
    span = length // 16
    count_b = out_len // 16
    window_sum = block_sum[:, :, 0:count_b]
    for index in range(1, span):
        window_sum = window_sum + block_sum[:, :, index:index + count_b]
    energy = window_sum[:, :, :, None] - prefix[:, :, :count_b, :] + prefix[:, :, span:span + count_b, :]
    energy = energy.reshape(count_w, chans, out_len)
    return lax.rsqrt(jnp.maximum(energy, 16.0))

def detect(window, window_scale, weighted, length):
    chans, total = window.shape
    out_len = total - length + 1
    width = math.gcd(out_len, 256)
    count = weighted.shape[0]

    def one_part(index):
        begin = (index * width).astype(jnp.int32)
        piece = lax.dynamic_slice_in_dim(window, begin, width + length - 1, 1)
        frames = jnp.stack([piece[:, lag:lag + width] for lag in range(length)], axis=1)
        part_scale = lax.dynamic_slice_in_dim(window_scale, begin, width, 1)
        framed = (frames.astype(jnp.float32) * part_scale[:, None, :]).astype(jnp.bfloat16)
        framed = framed.reshape(chans * length, width)
        return jnp.dot(weighted, framed, preferred_element_type=jnp.float32)
    parts = lax.map(one_part, jnp.arange(out_len // width, dtype=jnp.int32))
    return jnp.transpose(parts, (1, 0, 2)).reshape(count, out_len)

def reference(records, templates):
    length = templates.shape[2]
    padding = jnp.zeros((records.shape[0], records.shape[1], length - 1), records.dtype)
    extended = jnp.concatenate([records, padding], axis=2)
    weighted = make_weighted(templates)

    def one_window(window):
        scale = sliding_scale(window[None], length)[0]
        return detect(window, scale, weighted, length)
    return lax.map(one_window, extended)
```

```python
import functools

import jax
import jax.numpy as jnp
from jax import lax
from jax.experimental import pallas as pl
from jax.experimental.pallas import tpu as pltpu
from jax.sharding import PartitionSpec as P

MESH = pl.DeviceIdType.MESH
LANES = 128


def kernel(
    n, n_tm, rec_ref, tmp_ref, out_ref, wall, wf, ext, xf, scale, g, res,
    wsend, wrecv, hsend, hrecv, osend, orecv,
):
    me = lax.axis_index("tmpl")
    tm = lax.axis_index("tm")
    left = lax.rem(tm + n_tm - 1, n_tm)
    right = lax.rem(tm + 1, n_tm)
    chans, slab = rec_ref.shape
    rows, length = tmp_ref.shape
    own_k = rows // chans
    chunks = (slab + length) // LANES
    halves = length // LANES
    own_blocks = slab // LANES

    barrier = pltpu.get_barrier_semaphore()
    for d in range(1, n):
        pl.semaphore_signal(barrier, inc=1, device_id=(lax.rem(me + d, n), tm), device_id_type=MESH)
    for other in (left, right):
        pl.semaphore_signal(barrier, inc=1, device_id=(me, other), device_id_type=MESH)

    wide = tmp_ref[...].astype(jnp.float32)
    tinv = lax.rsqrt(jnp.sum(wide * wide, axis=1, keepdims=True) + 1e-06)
    weighted = (wide * tinv).astype(jnp.bfloat16)
    row = lax.broadcasted_iota(jnp.int32, (LANES, LANES), 0)
    col = lax.broadcasted_iota(jnp.int32, (LANES, LANES), 1)
    flip = jnp.where(row + col == LANES - 1, 1.0, 0.0).astype(jnp.bfloat16)
    for j in range(halves):
        part = weighted[:, j * LANES : (j + 1) * LANES]
        wall[me, :, j * LANES : (j + 1) * LANES] = jnp.dot(
            part, flip, preferred_element_type=jnp.float32
        ).astype(jnp.bfloat16)

    pl.semaphore_wait(barrier, n + 1)

    halo = pltpu.make_async_remote_copy(
        src_ref=rec_ref.at[:, pl.ds(0, length)], dst_ref=ext, send_sem=hsend, recv_sem=hrecv,
        device_id=(me, left), device_id_type=MESH,
    )
    halo.start()
    sends = []
    for d in range(1, n):
        copy = pltpu.make_async_remote_copy(
            src_ref=wall.at[me], dst_ref=wall.at[me], send_sem=wsend.at[d], recv_sem=wrecv.at[d],
            device_id=(lax.rem(me + d, n), tm), device_id_type=MESH,
        )
        copy.start()
        sends.append(copy)

    keep = col <= row

    def build(first, last):
        def group(index, carry):
            start = pl.multiple_of(index * 8, 8)
            lines = xf[pl.ds(start, 8), first * LANES : (last + 1) * LANES]
            for s in range(8):
                turned = []
                for m in range(last + 1 - first):
                    line = jnp.broadcast_to(lines[s : s + 1, m * LANES : (m + 1) * LANES], (LANES, LANES))
                    turned.append(pltpu.roll(line, 1, 1, stride=1, stride_axis=0))
                for m in range(first, last):
                    block = jnp.where(keep, turned[m - first], turned[m - first + 1])
                    g[start + s, :, m * LANES : (m + 1) * LANES] = block.astype(jnp.bfloat16)
            return carry

        lax.fori_loop(0, chans // 8, group, 0)

    xf[:, :slab] = rec_ref[...].astype(jnp.float32)
    build(0, own_blocks - 1)

    halo.wait()
    borrowed = ext[...].astype(jnp.float32)
    xf[:, slab:] = jnp.where(tm == n_tm - 1, 0.0, borrowed)
    build(own_blocks - 1, chunks - 1)

    def energies(index, carry):
        at = pl.ds(pl.multiple_of(index * 8, 8), 8)
        total = xf[at, :]
        total = total * total
        step = 1
        while step < LANES:
            total = total + pltpu.roll(total, slab + length - step, 1)
            step *= 2
        energy = total[:, :slab]
        for j in range(1, halves):
            energy = energy + total[:, j * LANES : j * LANES + slab]
        scale[at, :] = lax.rsqrt(jnp.maximum(energy, 16.0))
        return carry

    lax.fori_loop(0, chans // 8, energies, 0)

    for d in range(1, n):
        source = lax.rem(me + n - d, n)
        pltpu.make_async_remote_copy(
            src_ref=wall.at[source], dst_ref=wall.at[source], send_sem=wsend.at[d], recv_sem=wrecv.at[d],
            device_id=(source, tm), device_id_type=MESH,
        ).wait_recv()
    for i in range(n):
        for j in range(halves):
            wf[j, i * rows : (i + 1) * rows, :] = wall[i, :, j * LANES : (j + 1) * LANES].astype(jnp.float32)

    def channels(index, acc):
        start = pl.multiple_of(index * 8, 8)
        scales = scale[pl.ds(start, 8), :]
        for s in range(8):
            c = start + s
            lhs = jnp.concatenate(
                [wf[j, pl.ds(c, n * own_k, stride=chans), :] for j in range(halves)], axis=1
            ).astype(jnp.bfloat16)
            frames = jnp.concatenate([g[c, :, j * LANES : j * LANES + slab] for j in range(halves)], axis=0)
            part = jnp.dot(lhs, frames, preferred_element_type=jnp.float32)
            acc = acc + part * scales[s : s + 1, :]
        return acc

    acc = lax.fori_loop(0, chans // 8, channels, jnp.zeros((n * own_k, slab), jnp.float32))
    for i in range(n):
        res[i] = acc[i * own_k : (i + 1) * own_k, :]

    results = []
    for d in range(1, n):
        peer = lax.rem(me + d, n)
        copy = pltpu.make_async_remote_copy(
            src_ref=res.at[peer], dst_ref=out_ref.at[me], send_sem=osend.at[d], recv_sem=orecv.at[d],
            device_id=(peer, tm), device_id_type=MESH,
        )
        copy.start()
        results.append(copy)
    out_ref[me] = res[me]
    for copy in sends:
        copy.wait_send()
    for d in range(1, n):
        results[d - 1].wait_send()
        source = lax.rem(me + n - d, n)
        pltpu.make_async_remote_copy(
            src_ref=res.at[source], dst_ref=out_ref.at[source], send_sem=osend.at[d], recv_sem=orecv.at[d],
            device_id=(source, tm), device_id_type=MESH,
        ).wait_recv()


def solution(mesh):
    n, n_tm = mesh.shape["tmpl"], mesh.shape["tm"]

    def local(records, templates):
        _, chans, slab = records.shape
        own_k, _, length = templates.shape
        rows = own_k * chans
        return pl.pallas_call(
            functools.partial(kernel, n, n_tm),
            out_shape=jax.ShapeDtypeStruct((n, own_k, slab), jnp.float32),
            in_specs=[pl.BlockSpec(memory_space=pltpu.VMEM)] * 2,
            out_specs=pl.BlockSpec(memory_space=pltpu.VMEM),
            scratch_shapes=[
                pltpu.VMEM((n, rows, length), jnp.bfloat16),
                pltpu.VMEM((length // LANES, n * rows, LANES), jnp.float32),
                pltpu.VMEM((chans, length), jnp.bfloat16),
                pltpu.VMEM((chans, slab + length), jnp.float32),
                pltpu.VMEM((chans, slab), jnp.float32),
                pltpu.VMEM((chans, LANES, slab + length - LANES), jnp.bfloat16),
                pltpu.VMEM((n, own_k, slab), jnp.float32),
                pltpu.SemaphoreType.DMA((n,)),
                pltpu.SemaphoreType.DMA((n,)),
                pltpu.SemaphoreType.DMA,
                pltpu.SemaphoreType.DMA,
                pltpu.SemaphoreType.DMA((n,)),
                pltpu.SemaphoreType.DMA((n,)),
            ],
            compiler_params=pltpu.CompilerParams(
                collective_id=0, has_side_effects=True, vmem_limit_bytes=40 * 2**20
            ),
        )(records.reshape(chans, slab), templates.reshape(rows, length))

    placed = (P("tmpl", None, "tm"), P("tmpl", None, None))
    return jax.shard_map(
        local, mesh=mesh, in_specs=placed, out_specs=P(None, "tmpl", "tm"), check_vma=False
    )
```

```python
import functools

import jax
import jax.numpy as jnp
from jax import lax
from jax.experimental import pallas as pl
from jax.experimental.pallas import tpu as pltpu
from jax.sharding import PartitionSpec as P

MESH = pl.DeviceIdType.MESH
LANES = 128
SEED = 128


def kernel(
    n, n_tm, parts, rec_hbm, tmp_hbm, out_ref, rec_ref, tmp_ref, wall, wf, ext, xf, scale, g, res,
    insem, hsend, hrecv, zsend, zrecv, xsend, xrecv, csend, crecv, osend, orecv,
):
    me = lax.axis_index("tmpl")
    tm = lax.axis_index("tm")
    left = lax.rem(tm + n_tm - 1, n_tm)
    right = lax.rem(tm + 1, n_tm)
    chans, slab = rec_ref.shape
    rows, length = tmp_ref.shape
    own_k = rows // chans
    chunks = (slab + length) // LANES
    halves = length // LANES
    own_blocks = slab // LANES

    load_tmp = pltpu.make_async_copy(tmp_hbm, tmp_ref, insem.at[0])
    load_rec = pltpu.make_async_copy(rec_hbm, rec_ref, insem.at[1])
    load_tmp.start()
    load_rec.start()

    core = lax.rem(tm, 2)
    sibling = tm + 1 - 2 * core
    chip = lax.rem(tm // 2, 2)
    across = tm + 2 - 4 * chip
    share = rows // parts
    mine = core if parts == 2 else chip * 2 + core
    theirs = (1 - chip) * 2 + core

    barrier = pltpu.get_barrier_semaphore()
    for d in range(1, n):
        pl.semaphore_signal(barrier, inc=1, device_id=(lax.rem(me + d, n), tm), device_id_type=MESH)
    others = (left, right) if parts == 2 else (left, right, across)
    for other in others:
        pl.semaphore_signal(barrier, inc=1, device_id=(me, other), device_id_type=MESH)

    def block(e):
        return lax.rem(me + n - e, n)

    sent = []

    def piece(which, part, send_sem, recv_sem, to):
        at = wall.at[which, pl.ds(pl.multiple_of(part * share, share), share), :]
        return pltpu.make_async_remote_copy(
            src_ref=at, dst_ref=at, send_sem=send_sem, recv_sem=recv_sem, device_id=to, device_id_type=MESH
        )

    def send(*what):
        copy = piece(*what)
        copy.start()
        sent.append(copy)

    def to_peer(e):
        send(me, mine, zsend.at[e], zrecv.at[e], (lax.rem(me + e, n), tm))

    def to_x(e):
        if parts == 4:
            send(block(e), mine, xsend.at[e], xrecv.at[e], (me, across))

    def to_core(e, part, k):
        i = 2 * e + k
        send(block(e), part, csend.at[i], crecv.at[i], (me, sibling))

    def stage_peers():
        for e in range(1, n):
            to_peer(e)

    def stage_group():
        for e in range(1, n):
            piece(block(e), mine, zsend.at[e], zrecv.at[e], (me, tm)).wait_recv()
            to_x(e)
            to_core(e, mine, 0)

    def stage_core():
        if parts == 4:
            for e in range(1, n):
                piece(block(e), theirs, xsend.at[e], xrecv.at[e], (me, across)).wait_recv()
                to_core(e, theirs, 1)

    def stage_end():
        for e in range(1, n):
            for k in range(parts // 2):
                i = 2 * e + k
                if parts == 2:
                    part = 1 - core
                else:
                    part = (chip if k == 0 else 1 - chip) * 2 + 1 - core
                piece(block(e), part, csend.at[i], crecv.at[i], (me, sibling)).wait_recv()

    load_tmp.wait()
    wide = tmp_ref[...].astype(jnp.float32)
    tinv = lax.rsqrt(jnp.sum(wide * wide, axis=1, keepdims=True) + 1e-06)
    weighted = (wide * tinv).astype(jnp.bfloat16)
    row = lax.broadcasted_iota(jnp.int32, (LANES, LANES), 0)
    col = lax.broadcasted_iota(jnp.int32, (LANES, LANES), 1)
    flip = jnp.where(row + col == LANES - 1, 1.0, 0.0).astype(jnp.bfloat16)
    for j in range(halves):
        part = weighted[:, j * LANES : (j + 1) * LANES]
        wall[me, :, j * LANES : (j + 1) * LANES] = jnp.dot(
            part, flip, preferred_element_type=jnp.float32
        ).astype(jnp.bfloat16)

    pl.semaphore_wait(barrier, n - 1 + len(others))
    stage_peers()
    load_rec.wait()
    halo = pltpu.make_async_remote_copy(
        src_ref=rec_ref.at[:, pl.ds(0, length)], dst_ref=ext, send_sem=hsend, recv_sem=hrecv,
        device_id=(me, left), device_id_type=MESH,
    )
    halo.start()

    seed_row = lax.broadcasted_iota(jnp.int32, (SEED, LANES), 0)
    seed_col = lax.broadcasted_iota(jnp.int32, (SEED, LANES), 1)
    keep = seed_col + (SEED - 1) - seed_row < LANES

    def shifted(pieces, step):
        lane = lax.broadcasted_iota(jnp.int32, pieces[0].shape, 1)
        moved = [pltpu.roll(piece, LANES - step, 1) for piece in pieces]
        last = len(pieces) - 1
        return [jnp.where(lane < LANES - step, moved[m], moved[min(m + 1, last)]) for m in range(last + 1)]

    def frames_of(lines, s, count):
        turned = []
        for m in range(count):
            line = jnp.broadcast_to(lines[s : s + 1, m * LANES : (m + 1) * LANES], (SEED, LANES))
            turned.append(pltpu.roll(line, LANES - SEED + 1, 1, stride=1, stride_axis=0))
        block = [
            jnp.where(keep, turned[m], turned[min(m + 1, count - 1)]).astype(jnp.bfloat16)
            for m in range(count)
        ]
        step = SEED
        while step < LANES:
            ahead = shifted(block, step)
            block = [jnp.concatenate([ahead[m], block[m]], axis=0) for m in range(count)]
            step *= 2
        return block

    def build(start, first, last):
        lines = xf[pl.ds(start, 8), first * LANES : (last + 1) * LANES]
        for s in range(8):
            block = frames_of(lines, s, last + 1 - first)
            for m in range(first, last):
                g[start + s, :, m * LANES : (m + 1) * LANES] = block[m - first]

    def energies():
        total = [xf[:, m * LANES : (m + 1) * LANES] for m in range(chunks)]
        total = [piece * piece for piece in total]
        step = 1
        while step < LANES:
            total = [piece + later for piece, later in zip(total, shifted(total, step))]
            step *= 2
        energy = jnp.concatenate([sum(total[m + 1 : m + halves], total[m]) for m in range(own_blocks)], axis=1)
        scale[...] = lax.rsqrt(jnp.maximum(energy, 16.0))

    def own_part(index, carry):
        build(pl.multiple_of(index * 8, 8), 0, own_blocks - 1)
        return carry

    def rest(index, carry):
        start = pl.multiple_of(index * 8, 8)
        build(start, own_blocks - 1, chunks - 1)
        return carry

    xf[:, :slab] = rec_ref[...].astype(jnp.float32)
    lax.fori_loop(0, chans // 8, own_part, 0)
    halo.wait()
    borrowed = ext[...].astype(jnp.float32)
    xf[:, slab:] = jnp.where(tm == n_tm - 1, 0.0, borrowed)
    lax.fori_loop(0, chans // 8, rest, 0)
    stage_group()
    energies()
    stage_core()
    stage_end()
    for i in range(n):
        for j in range(halves):
            wf[j, i * rows : (i + 1) * rows, :] = wall[i, :, j * LANES : (j + 1) * LANES].astype(jnp.float32)

    def channels(index, acc):
        start = pl.multiple_of(index * 8, 8)
        scales = scale[pl.ds(start, 8), :]
        for s in range(8):
            c = start + s
            lhs = jnp.concatenate(
                [wf[j, pl.ds(c, n * own_k, stride=chans), :] for j in range(halves)], axis=0
            ).astype(jnp.bfloat16)
            sums = jnp.dot(lhs, g[c], preferred_element_type=jnp.float32)
            part = sums[: n * own_k, :slab]
            for j in range(1, halves):
                part = part + sums[j * n * own_k : (j + 1) * n * own_k, j * LANES : j * LANES + slab]
            acc = acc + part * scales[s : s + 1, :]
        return acc

    acc = lax.fori_loop(0, chans // 8, channels, jnp.zeros((n * own_k, slab), jnp.float32))
    for i in range(n):
        res[i] = acc[i * own_k : (i + 1) * own_k, :]

    results = []
    for d in range(1, n):
        peer = lax.rem(me + d, n)
        copy = pltpu.make_async_remote_copy(
            src_ref=res.at[peer], dst_ref=out_ref.at[me], send_sem=osend.at[d], recv_sem=orecv.at[d],
            device_id=(peer, tm), device_id_type=MESH,
        )
        copy.start()
        results.append(copy)
    out_ref[me] = res[me]
    for copy in sent:
        copy.wait_send()
    for d in range(1, n):
        results[d - 1].wait_send()
        source = lax.rem(me + n - d, n)
        pltpu.make_async_remote_copy(
            src_ref=res.at[source], dst_ref=out_ref.at[source], send_sem=osend.at[d], recv_sem=orecv.at[d],
            device_id=(source, tm), device_id_type=MESH,
        ).wait_recv()


def solution(mesh):
    n, n_tm = mesh.shape["tmpl"], mesh.shape["tm"]
    parts = 2

    def local(records, templates):
        _, chans, slab = records.shape
        own_k, _, length = templates.shape
        rows = own_k * chans
        return pl.pallas_call(
            functools.partial(kernel, n, n_tm, parts),
            out_shape=jax.ShapeDtypeStruct((n, own_k, slab), jnp.float32),
            in_specs=[pl.BlockSpec(memory_space=pl.ANY)] * 2,
            out_specs=pl.BlockSpec(memory_space=pltpu.VMEM),
            scratch_shapes=[
                pltpu.VMEM((chans, slab), jnp.bfloat16),
                pltpu.VMEM((rows, length), jnp.bfloat16),
                pltpu.VMEM((n, rows, length), jnp.bfloat16),
                pltpu.VMEM((length // LANES, n * rows, LANES), jnp.float32),
                pltpu.VMEM((chans, length), jnp.bfloat16),
                pltpu.VMEM((chans, slab + length), jnp.float32),
                pltpu.VMEM((chans, slab), jnp.float32),
                pltpu.VMEM((chans, LANES, slab + length - LANES), jnp.bfloat16),
                pltpu.VMEM((n, own_k, slab), jnp.float32),
                pltpu.SemaphoreType.DMA((2,)),
                pltpu.SemaphoreType.DMA,
                pltpu.SemaphoreType.DMA,
                pltpu.SemaphoreType.DMA((n,)),
                pltpu.SemaphoreType.DMA((n,)),
                pltpu.SemaphoreType.DMA((n,)),
                pltpu.SemaphoreType.DMA((n,)),
                pltpu.SemaphoreType.DMA((2 * n,)),
                pltpu.SemaphoreType.DMA((2 * n,)),
                pltpu.SemaphoreType.DMA((n,)),
                pltpu.SemaphoreType.DMA((n,)),
            ],
            compiler_params=pltpu.CompilerParams(
                collective_id=0, has_side_effects=True, vmem_limit_bytes=40 * 2**20
            ),
        )(records.reshape(chans, slab), templates.reshape(rows, length))

    placed = (P("tmpl", None, "tm"), P("tmpl", None, None))
    return jax.shard_map(
        local, mesh=mesh, in_specs=placed, out_specs=P(None, "tmpl", "tm"), check_vma=False
    )
```

```python
import functools

import jax
import jax.numpy as jnp
from jax import lax
from jax.experimental import pallas as pl
from jax.experimental.pallas import tpu as pltpu
from jax.sharding import PartitionSpec as P

MESH = pl.DeviceIdType.MESH
LANES = 128
SEED = 128


def kernel(
    n, n_tm, parts, rec_hbm, tmp_hbm, out_ref, rec_ref, tmp_ref, wall, wf, ext, xf, scale, g, res,
    insem, hsend, hrecv, zsend, zrecv, xsend, xrecv, csend, crecv, osend, orecv,
):
    me = lax.axis_index("tmpl")
    tm = lax.axis_index("tm")
    left = lax.rem(tm + n_tm - 1, n_tm)
    right = lax.rem(tm + 1, n_tm)
    chans, slab = rec_ref.shape
    rows, length = tmp_ref.shape
    own_k = rows // chans
    chunks = (slab + length) // LANES
    halves = length // LANES
    own_blocks = slab // LANES

    load_tmp = pltpu.make_async_copy(tmp_hbm, tmp_ref, insem.at[0])
    load_rec = pltpu.make_async_copy(rec_hbm, rec_ref, insem.at[1])
    load_tmp.start()
    load_rec.start()

    core = lax.rem(tm, 2)
    sibling = tm + 1 - 2 * core
    chip = lax.rem(tm // 2, 2)
    across = tm + 2 - 4 * chip
    share = chans // parts
    mine = core if parts == 2 else chip * 2 + core
    theirs = (1 - chip) * 2 + core

    barrier = pltpu.get_barrier_semaphore()
    for d in range(1, n):
        pl.semaphore_signal(barrier, inc=1, device_id=(lax.rem(me + d, n), tm), device_id_type=MESH)
    others = (left, right) if parts == 2 else (left, right, across)
    for other in others:
        pl.semaphore_signal(barrier, inc=1, device_id=(me, other), device_id_type=MESH)

    def block(e):
        return lax.rem(me + n - e, n)

    sent = []

    def piece(which, part, send_sem, recv_sem, to):
        at = wall.at[which, part]
        return pltpu.make_async_remote_copy(
            src_ref=at, dst_ref=at, send_sem=send_sem, recv_sem=recv_sem, device_id=to, device_id_type=MESH
        )

    def send(*what):
        copy = piece(*what)
        copy.start()
        sent.append(copy)

    def to_peer(e):
        send(me, mine, zsend.at[e], zrecv.at[e], (lax.rem(me + e, n), tm))

    def to_x(e):
        if parts == 4:
            send(block(e), mine, xsend.at[e], xrecv.at[e], (me, across))

    def to_core(e, part, k):
        i = 2 * e + k
        send(block(e), part, csend.at[i], crecv.at[i], (me, sibling))

    def stage_peers():
        for e in range(n - 1, 0, -1):
            to_peer(e)

    def stage_group():
        for e in range(1, n):
            piece(block(e), mine, zsend.at[e], zrecv.at[e], (me, tm)).wait_recv()
            to_x(e)
            to_core(e, mine, 0)

    def stage_core():
        if parts == 4:
            for e in range(1, n):
                piece(block(e), theirs, xsend.at[e], xrecv.at[e], (me, across)).wait_recv()
                to_core(e, theirs, 1)

    def stage_end(k):
        for e in range(1, n):
            i = 2 * e + k
            if parts == 2:
                part = 1 - core
            else:
                part = (chip if k == 0 else 1 - chip) * 2 + 1 - core
            piece(block(e), part, csend.at[i], crecv.at[i], (me, sibling)).wait_recv()

    load_tmp.wait()
    wide = tmp_ref[...].astype(jnp.float32)
    tinv = lax.rsqrt(jnp.sum(wide * wide, axis=1, keepdims=True) + 1e-06)
    weighted = (wide * tinv).astype(jnp.bfloat16)
    row = lax.broadcasted_iota(jnp.int32, (LANES, LANES), 0)
    col = lax.broadcasted_iota(jnp.int32, (LANES, LANES), 1)
    flip = jnp.where(row + col == LANES - 1, 1.0, 0.0).astype(jnp.bfloat16)
    for j in range(halves):
        part = weighted[:, j * LANES : (j + 1) * LANES]
        turned = jnp.dot(part, flip, preferred_element_type=jnp.float32).astype(jnp.bfloat16)
        for q in range(parts):
            for k in range(own_k):
                at = k * chans + q * share
                wall[me, q, k * share : (k + 1) * share, j * LANES : (j + 1) * LANES] = turned[at : at + share]

    pl.semaphore_wait(barrier, n - 1 + len(others))
    stage_peers()
    load_rec.wait()
    halo = pltpu.make_async_remote_copy(
        src_ref=rec_ref.at[:, pl.ds(0, length)], dst_ref=ext, send_sem=hsend, recv_sem=hrecv,
        device_id=(me, left), device_id_type=MESH,
    )
    halo.start()

    seed_row = lax.broadcasted_iota(jnp.int32, (SEED, LANES), 0)
    seed_col = lax.broadcasted_iota(jnp.int32, (SEED, LANES), 1)
    keep = seed_col + (SEED - 1) - seed_row < LANES

    def shifted(pieces, step):
        lane = lax.broadcasted_iota(jnp.int32, pieces[0].shape, 1)
        moved = [pltpu.roll(piece, LANES - step, 1) for piece in pieces]
        last = len(pieces) - 1
        return [jnp.where(lane < LANES - step, moved[m], moved[min(m + 1, last)]) for m in range(last + 1)]

    def frames_of(lines, s, count):
        turned = []
        for m in range(count):
            line = jnp.broadcast_to(lines[s : s + 1, m * LANES : (m + 1) * LANES], (SEED, LANES))
            turned.append(pltpu.roll(line, LANES - SEED + 1, 1, stride=1, stride_axis=0))
        block = [
            jnp.where(keep, turned[m], turned[min(m + 1, count - 1)]).astype(jnp.bfloat16)
            for m in range(count)
        ]
        step = SEED
        while step < LANES:
            ahead = shifted(block, step)
            block = [jnp.concatenate([ahead[m], block[m]], axis=0) for m in range(count)]
            step *= 2
        return block

    def build(start, first, last):
        lines = xf[pl.ds(start, 8), first * LANES : (last + 1) * LANES]
        for s in range(8):
            block = frames_of(lines, s, last + 1 - first)
            for m in range(first, last):
                g[start + s, :, m * LANES : (m + 1) * LANES] = block[m - first]

    def energies():
        total = [xf[:, m * LANES : (m + 1) * LANES] for m in range(chunks)]
        total = [piece * piece for piece in total]
        step = 1
        while step < LANES:
            total = [piece + later for piece, later in zip(total, shifted(total, step))]
            step *= 2
        energy = jnp.concatenate([sum(total[m + 1 : m + halves], total[m]) for m in range(own_blocks)], axis=1)
        scale[...] = lax.rsqrt(jnp.maximum(energy, 16.0))

    def own_part(index, carry):
        build(pl.multiple_of(index * 8, 8), 0, own_blocks - 1)
        return carry

    def rest(index, carry):
        start = pl.multiple_of(index * 8, 8)
        build(start, own_blocks - 1, chunks - 1)
        return carry

    def whole(index, carry):
        build(pl.multiple_of(index * 8, 8), 0, chunks - 1)
        return carry

    xf[:, :slab] = rec_ref[...].astype(jnp.float32)
    early = chans // 16
    lax.fori_loop(0, early, own_part, 0)
    halo.wait()
    borrowed = ext[...].astype(jnp.float32)
    xf[:, slab:] = jnp.where(tm == n_tm - 1, 0.0, borrowed)
    lax.fori_loop(0, early, rest, 0)
    lax.fori_loop(early, chans // 8, whole, 0)
    stage_group()
    energies()

    size = own_k * share

    def widen(part):
        for i in range(n):
            start = pl.multiple_of((part * n + i) * size, size)
            for j in range(halves):
                wf[j, pl.ds(start, size), :] = wall[i, part, :, j * LANES : (j + 1) * LANES].astype(jnp.float32)

    def channels(part, index, acc):
        start = pl.multiple_of(part * share + index * 8, 8)
        scales = scale[pl.ds(start, 8), :]
        base = pl.multiple_of(part * n * size + index * 8, 8)
        for s in range(8):
            lhs = jnp.concatenate(
                [wf[j, pl.ds(base + s, n * own_k, stride=share), :] for j in range(halves)], axis=0
            ).astype(jnp.bfloat16)
            sums = jnp.dot(lhs, g[start + s], preferred_element_type=jnp.float32)
            total = sums[: n * own_k, :slab]
            for j in range(1, halves):
                total = total + sums[j * n * own_k : (j + 1) * n * own_k, j * LANES : j * LANES + slab]
            acc = acc + total * scales[s : s + 1, :]
        return acc

    def correlate(part, acc):
        widen(part)
        return lax.fori_loop(0, share // 8, functools.partial(channels, part), acc)

    acc = correlate(mine, jnp.zeros((n * own_k, slab), jnp.float32))
    stage_core()
    if parts == 4:
        acc = correlate(theirs, acc)
    stage_end(0)
    acc = correlate(1 - core if parts == 2 else chip * 2 + 1 - core, acc)
    if parts == 4:
        stage_end(1)
        acc = correlate((1 - chip) * 2 + 1 - core, acc)
    for i in range(n):
        res[i] = acc[i * own_k : (i + 1) * own_k, :]

    results = []
    for d in range(1, n):
        peer = lax.rem(me + d, n)
        copy = pltpu.make_async_remote_copy(
            src_ref=res.at[peer], dst_ref=out_ref.at[me], send_sem=osend.at[d], recv_sem=orecv.at[d],
            device_id=(peer, tm), device_id_type=MESH,
        )
        copy.start()
        results.append(copy)
    out_ref[me] = res[me]
    for copy in sent:
        copy.wait_send()
    for d in range(1, n):
        results[d - 1].wait_send()
        source = lax.rem(me + n - d, n)
        pltpu.make_async_remote_copy(
            src_ref=res.at[source], dst_ref=out_ref.at[source], send_sem=osend.at[d], recv_sem=orecv.at[d],
            device_id=(source, tm), device_id_type=MESH,
        ).wait_recv()


def solution(mesh):
    n, n_tm = mesh.shape["tmpl"], mesh.shape["tm"]
    parts = 2

    def local(records, templates):
        _, chans, slab = records.shape
        own_k, _, length = templates.shape
        rows = own_k * chans
        return pl.pallas_call(
            functools.partial(kernel, n, n_tm, parts),
            out_shape=jax.ShapeDtypeStruct((n, own_k, slab), jnp.float32),
            in_specs=[pl.BlockSpec(memory_space=pl.ANY)] * 2,
            out_specs=pl.BlockSpec(memory_space=pltpu.VMEM),
            scratch_shapes=[
                pltpu.VMEM((chans, slab), jnp.bfloat16),
                pltpu.VMEM((rows, length), jnp.bfloat16),
                pltpu.VMEM((n, parts, rows // parts, length), jnp.bfloat16),
                pltpu.VMEM((length // LANES, n * rows, LANES), jnp.float32),
                pltpu.VMEM((chans, length), jnp.bfloat16),
                pltpu.VMEM((chans, slab + length), jnp.float32),
                pltpu.VMEM((chans, slab), jnp.float32),
                pltpu.VMEM((chans, LANES, slab + length - LANES), jnp.bfloat16),
                pltpu.VMEM((n, own_k, slab), jnp.float32),
                pltpu.SemaphoreType.DMA((2,)),
                pltpu.SemaphoreType.DMA,
                pltpu.SemaphoreType.DMA,
                pltpu.SemaphoreType.DMA((n,)),
                pltpu.SemaphoreType.DMA((n,)),
                pltpu.SemaphoreType.DMA((n,)),
                pltpu.SemaphoreType.DMA((n,)),
                pltpu.SemaphoreType.DMA((2 * n,)),
                pltpu.SemaphoreType.DMA((2 * n,)),
                pltpu.SemaphoreType.DMA((n,)),
                pltpu.SemaphoreType.DMA((n,)),
            ],
            compiler_params=pltpu.CompilerParams(
                collective_id=0, has_side_effects=True, vmem_limit_bytes=40 * 2**20
            ),
        )(records.reshape(chans, slab), templates.reshape(rows, length))

    placed = (P("tmpl", None, "tm"), P("tmpl", None, None))
    return jax.shard_map(
        local, mesh=mesh, in_specs=placed, out_specs=P(None, "tmpl", "tm"), check_vma=False
    )
```

```python
import functools

import jax
import jax.numpy as jnp
from jax import lax
from jax.experimental import pallas as pl
from jax.experimental.pallas import tpu as pltpu
from jax.sharding import PartitionSpec as P

MESH = pl.DeviceIdType.MESH
LANES = 128
SEED = 128


def kernel(
    n, n_tm, parts, rec_hbm, tmp_hbm, out_ref, rec_ref, tmp_ref, wall, wf, ext, xf, scale, g, res,
    insem, hsend, hrecv, zsend, zrecv, xsend, xrecv, csend, crecv, osend, orecv,
):
    me = lax.axis_index("tmpl")
    tm = lax.axis_index("tm")
    left = lax.rem(tm + n_tm - 1, n_tm)
    right = lax.rem(tm + 1, n_tm)
    chans, slab = rec_ref.shape
    rows, length = tmp_ref.shape
    own_k = rows // chans
    chunks = (slab + length) // LANES
    halves = length // LANES
    own_blocks = slab // LANES

    load_tmp = pltpu.make_async_copy(tmp_hbm, tmp_ref, insem.at[0])
    load_rec = pltpu.make_async_copy(rec_hbm, rec_ref, insem.at[1])
    load_tmp.start()
    load_rec.start()

    core = lax.rem(tm, 2)
    sibling = tm + 1 - 2 * core
    chip = lax.rem(tm // 2, 2)
    across = tm + 2 - 4 * chip
    share = chans // parts
    mine = core if parts == 2 else chip * 2 + core
    theirs = (1 - chip) * 2 + core

    barrier = pltpu.get_barrier_semaphore()
    for d in range(1, n):
        pl.semaphore_signal(barrier, inc=1, device_id=(lax.rem(me + d, n), tm), device_id_type=MESH)
    others = (left, right) if parts == 2 else (left, right, across)
    for other in others:
        pl.semaphore_signal(barrier, inc=1, device_id=(me, other), device_id_type=MESH)

    def block(e):
        return lax.rem(me + n - e, n)

    sent = []

    def piece(which, part, send_sem, recv_sem, to):
        at = wall.at[which, part]
        return pltpu.make_async_remote_copy(
            src_ref=at, dst_ref=at, send_sem=send_sem, recv_sem=recv_sem, device_id=to, device_id_type=MESH
        )

    def send(*what):
        copy = piece(*what)
        copy.start()
        sent.append(copy)

    def to_peer(e):
        send(me, mine, zsend.at[e], zrecv.at[e], (lax.rem(me + e, n), tm))

    def to_x(e):
        if parts == 4:
            send(block(e), mine, xsend.at[e], xrecv.at[e], (me, across))

    def to_core(e, part, k):
        i = 2 * e + k
        send(block(e), part, csend.at[i], crecv.at[i], (me, sibling))

    def stage_peers():
        for e in range(n - 1, 0, -1):
            to_peer(e)

    def stage_group():
        for e in range(1, n):
            piece(block(e), mine, zsend.at[e], zrecv.at[e], (me, tm)).wait_recv()
            to_x(e)
            to_core(e, mine, 0)

    def stage_core():
        if parts == 4:
            for e in range(1, n):
                piece(block(e), theirs, xsend.at[e], xrecv.at[e], (me, across)).wait_recv()
                to_core(e, theirs, 1)

    def stage_end(k):
        for e in range(1, n):
            i = 2 * e + k
            if parts == 2:
                part = 1 - core
            else:
                part = (chip if k == 0 else 1 - chip) * 2 + 1 - core
            piece(block(e), part, csend.at[i], crecv.at[i], (me, sibling)).wait_recv()

    load_tmp.wait()
    wide = tmp_ref[...].astype(jnp.float32)
    tinv = lax.rsqrt(jnp.sum(wide * wide, axis=1, keepdims=True) + 1e-06)
    weighted = (wide * tinv).astype(jnp.bfloat16)
    row = lax.broadcasted_iota(jnp.int32, (LANES, LANES), 0)
    col = lax.broadcasted_iota(jnp.int32, (LANES, LANES), 1)
    flip = jnp.where(row + col == LANES - 1, 1.0, 0.0).astype(jnp.bfloat16)
    for j in range(halves):
        part = weighted[:, j * LANES : (j + 1) * LANES]
        turned = jnp.dot(part, flip, preferred_element_type=jnp.float32).astype(jnp.bfloat16)
        for q in range(parts):
            for k in range(own_k):
                at = k * chans + q * share
                wall[me, q, k * share : (k + 1) * share, j * LANES : (j + 1) * LANES] = turned[at : at + share]

    pl.semaphore_wait(barrier, n - 1 + len(others))
    stage_peers()
    load_rec.wait()
    halo = pltpu.make_async_remote_copy(
        src_ref=rec_ref.at[:, pl.ds(0, length)], dst_ref=ext, send_sem=hsend, recv_sem=hrecv,
        device_id=(me, left), device_id_type=MESH,
    )
    halo.start()

    seed_row = lax.broadcasted_iota(jnp.int32, (SEED, LANES), 0)
    seed_col = lax.broadcasted_iota(jnp.int32, (SEED, LANES), 1)
    keep = seed_col + (SEED - 1) - seed_row < LANES

    def shifted(pieces, step):
        lane = lax.broadcasted_iota(jnp.int32, pieces[0].shape, 1)
        moved = [pltpu.roll(piece, LANES - step, 1) for piece in pieces]
        last = len(pieces) - 1
        return [jnp.where(lane < LANES - step, moved[m], moved[min(m + 1, last)]) for m in range(last + 1)]

    def frames_of(lines, s, count):
        turned = []
        for m in range(count):
            line = jnp.broadcast_to(lines[s : s + 1, m * LANES : (m + 1) * LANES], (SEED, LANES))
            turned.append(pltpu.roll(line, LANES - SEED + 1, 1, stride=1, stride_axis=0))
        block = [
            jnp.where(keep, turned[m], turned[min(m + 1, count - 1)]).astype(jnp.bfloat16)
            for m in range(count)
        ]
        step = SEED
        while step < LANES:
            ahead = shifted(block, step)
            block = [jnp.concatenate([ahead[m], block[m]], axis=0) for m in range(count)]
            step *= 2
        return block

    def build(start, first, last):
        lines = xf[pl.ds(start, 8), first * LANES : (last + 1) * LANES]
        for s in range(8):
            block = frames_of(lines, s, last + 1 - first)
            for m in range(first, last):
                g[start + s, :, m * LANES : (m + 1) * LANES] = block[m - first]

    def energies():
        total = [xf[:, m * LANES : (m + 1) * LANES] for m in range(chunks)]
        total = [piece * piece for piece in total]
        step = 1
        while step < LANES:
            total = [piece + later for piece, later in zip(total, shifted(total, step))]
            step *= 2
        energy = jnp.concatenate([sum(total[m + 1 : m + halves], total[m]) for m in range(own_blocks)], axis=1)
        scale[...] = lax.rsqrt(jnp.maximum(energy, 16.0))

    def own_part(index, carry):
        build(pl.multiple_of(index * 8, 8), 0, own_blocks - 1)
        return carry

    def rest(index, carry):
        start = pl.multiple_of(index * 8, 8)
        build(start, own_blocks - 1, chunks - 1)
        return carry

    def whole(index, carry):
        build(pl.multiple_of(index * 8, 8), 0, chunks - 1)
        return carry

    xf[:, :slab] = rec_ref[...].astype(jnp.float32)
    early = chans // 16
    lax.fori_loop(0, early, own_part, 0)
    halo.wait()
    borrowed = ext[...].astype(jnp.float32)
    xf[:, slab:] = jnp.where(tm == n_tm - 1, 0.0, borrowed)
    lax.fori_loop(0, early, rest, 0)
    stage_group()
    lax.fori_loop(early, chans // 8, whole, 0)
    energies()

    size = own_k * share

    def widen(part):
        for i in range(n):
            start = pl.multiple_of((part * n + i) * size, size)
            for j in range(halves):
                wf[j, pl.ds(start, size), :] = wall[i, part, :, j * LANES : (j + 1) * LANES].astype(jnp.float32)

    def channels(part, index, acc):
        start = pl.multiple_of(part * share + index * 8, 8)
        scales = scale[pl.ds(start, 8), :]
        base = pl.multiple_of(part * n * size + index * 8, 8)
        for s in range(8):
            lhs = jnp.concatenate(
                [wf[j, pl.ds(base + s, n * own_k, stride=share), :] for j in range(halves)], axis=0
            ).astype(jnp.bfloat16)
            sums = jnp.dot(lhs, g[start + s], preferred_element_type=jnp.float32)
            total = sums[: n * own_k, :slab]
            for j in range(1, halves):
                total = total + sums[j * n * own_k : (j + 1) * n * own_k, j * LANES : j * LANES + slab]
            acc = acc + total * scales[s : s + 1, :]
        return acc

    def correlate(part, acc):
        widen(part)
        return lax.fori_loop(0, share // 8, functools.partial(channels, part), acc)

    acc = correlate(mine, jnp.zeros((n * own_k, slab), jnp.float32))
    stage_core()
    if parts == 4:
        acc = correlate(theirs, acc)
    stage_end(0)
    acc = correlate(1 - core if parts == 2 else chip * 2 + 1 - core, acc)
    if parts == 4:
        stage_end(1)
        acc = correlate((1 - chip) * 2 + 1 - core, acc)
    for i in range(n):
        res[i] = acc[i * own_k : (i + 1) * own_k, :]

    results = []
    for d in range(1, n):
        peer = lax.rem(me + d, n)
        copy = pltpu.make_async_remote_copy(
            src_ref=res.at[peer], dst_ref=out_ref.at[me], send_sem=osend.at[d], recv_sem=orecv.at[d],
            device_id=(peer, tm), device_id_type=MESH,
        )
        copy.start()
        results.append(copy)
    out_ref[me] = res[me]
    for copy in sent:
        copy.wait_send()
    for d in range(1, n):
        results[d - 1].wait_send()
        source = lax.rem(me + n - d, n)
        pltpu.make_async_remote_copy(
            src_ref=res.at[source], dst_ref=out_ref.at[source], send_sem=osend.at[d], recv_sem=orecv.at[d],
            device_id=(source, tm), device_id_type=MESH,
        ).wait_recv()


def solution(mesh):
    n, n_tm = mesh.shape["tmpl"], mesh.shape["tm"]
    parts = 4

    def local(records, templates):
        _, chans, slab = records.shape
        own_k, _, length = templates.shape
        rows = own_k * chans
        return pl.pallas_call(
            functools.partial(kernel, n, n_tm, parts),
            out_shape=jax.ShapeDtypeStruct((n, own_k, slab), jnp.float32),
            in_specs=[pl.BlockSpec(memory_space=pl.ANY)] * 2,
            out_specs=pl.BlockSpec(memory_space=pltpu.VMEM),
            scratch_shapes=[
                pltpu.VMEM((chans, slab), jnp.bfloat16),
                pltpu.VMEM((rows, length), jnp.bfloat16),
                pltpu.VMEM((n, parts, rows // parts, length), jnp.bfloat16),
                pltpu.VMEM((length // LANES, n * rows, LANES), jnp.float32),
                pltpu.VMEM((chans, length), jnp.bfloat16),
                pltpu.VMEM((chans, slab + length), jnp.float32),
                pltpu.VMEM((chans, slab), jnp.float32),
                pltpu.VMEM((chans, LANES, slab + length - LANES), jnp.bfloat16),
                pltpu.VMEM((n, own_k, slab), jnp.float32),
                pltpu.SemaphoreType.DMA((2,)),
                pltpu.SemaphoreType.DMA,
                pltpu.SemaphoreType.DMA,
                pltpu.SemaphoreType.DMA((n,)),
                pltpu.SemaphoreType.DMA((n,)),
                pltpu.SemaphoreType.DMA((n,)),
                pltpu.SemaphoreType.DMA((n,)),
                pltpu.SemaphoreType.DMA((2 * n,)),
                pltpu.SemaphoreType.DMA((2 * n,)),
                pltpu.SemaphoreType.DMA((n,)),
                pltpu.SemaphoreType.DMA((n,)),
            ],
            compiler_params=pltpu.CompilerParams(
                collective_id=0, has_side_effects=True, vmem_limit_bytes=40 * 2**20
            ),
        )(records.reshape(chans, slab), templates.reshape(rows, length))

    placed = (P("tmpl", None, "tm"), P("tmpl", None, None))
    return jax.shard_map(
        local, mesh=mesh, in_specs=placed, out_specs=P(None, "tmpl", "tm"), check_vma=False
    )
```

```python
import functools

import jax
import jax.numpy as jnp
from jax import lax
from jax.experimental import pallas as pl
from jax.experimental.pallas import tpu as pltpu
from jax.sharding import PartitionSpec as P

MESH = pl.DeviceIdType.MESH
LANES = 128
SEED = 128


def kernel(
    n, n_tm, parts, rec_hbm, tmp_hbm, out_ref, rec_ref, tmp_ref, wall, wf, ext, xf, scale, g, res,
    insem, hsend, hrecv, zsend, zrecv, xsend, xrecv, csend, crecv, osend, orecv,
):
    me = lax.axis_index("tmpl")
    tm = lax.axis_index("tm")
    left = lax.rem(tm + n_tm - 1, n_tm)
    right = lax.rem(tm + 1, n_tm)
    chans, slab = rec_ref.shape
    rows, length = tmp_ref.shape
    own_k = rows // chans
    chunks = (slab + length) // LANES
    halves = length // LANES
    own_blocks = slab // LANES

    load_tmp = pltpu.make_async_copy(tmp_hbm, tmp_ref, insem.at[0])
    load_rec = pltpu.make_async_copy(rec_hbm, rec_ref, insem.at[1])
    load_tmp.start()
    load_rec.start()

    core = lax.rem(tm, 2)
    sibling = tm + 1 - 2 * core
    chip = lax.rem(tm // 2, 2)
    across = tm + 2 - 4 * chip
    share = chans // parts
    mine = core if parts == 2 else chip * 2 + core
    theirs = (1 - chip) * 2 + core

    barrier = pltpu.get_barrier_semaphore()
    for d in range(1, n):
        pl.semaphore_signal(barrier, inc=1, device_id=(lax.rem(me + d, n), tm), device_id_type=MESH)
    others = (left, right) if parts == 2 else (left, right, across)
    for other in others:
        pl.semaphore_signal(barrier, inc=1, device_id=(me, other), device_id_type=MESH)

    def block(e):
        return lax.rem(me + n - e, n)

    sent = []

    def piece(which, part, send_sem, recv_sem, to):
        at = wall.at[which, part]
        return pltpu.make_async_remote_copy(
            src_ref=at, dst_ref=at, send_sem=send_sem, recv_sem=recv_sem, device_id=to, device_id_type=MESH
        )

    def send(*what):
        copy = piece(*what)
        copy.start()
        sent.append(copy)

    def to_peer(e):
        send(me, mine, zsend.at[e], zrecv.at[e], (lax.rem(me + e, n), tm))

    def to_x(e):
        if parts == 4:
            send(block(e), mine, xsend.at[e], xrecv.at[e], (me, across))

    def to_core(e, part, k):
        i = 2 * e + k
        send(block(e), part, csend.at[i], crecv.at[i], (me, sibling))

    def stage_peers():
        for e in range(n - 1, 0, -1):
            to_peer(e)

    def stage_group():
        for e in range(1, n):
            piece(block(e), mine, zsend.at[e], zrecv.at[e], (me, tm)).wait_recv()
            to_x(e)
            to_core(e, mine, 0)

    def stage_core():
        if parts == 4:
            for e in range(1, n):
                piece(block(e), theirs, xsend.at[e], xrecv.at[e], (me, across)).wait_recv()
                to_core(e, theirs, 1)

    def stage_end(k):
        for e in range(1, n):
            i = 2 * e + k
            if parts == 2:
                part = 1 - core
            else:
                part = (chip if k == 0 else 1 - chip) * 2 + 1 - core
            piece(block(e), part, csend.at[i], crecv.at[i], (me, sibling)).wait_recv()

    load_tmp.wait()
    wide = tmp_ref[...].astype(jnp.float32)
    tinv = lax.rsqrt(jnp.sum(wide * wide, axis=1, keepdims=True) + 1e-06)
    weighted = (wide * tinv).astype(jnp.bfloat16)
    row = lax.broadcasted_iota(jnp.int32, (LANES, LANES), 0)
    col = lax.broadcasted_iota(jnp.int32, (LANES, LANES), 1)
    flip = jnp.where(row + col == LANES - 1, 1.0, 0.0).astype(jnp.bfloat16)
    for j in range(halves):
        part = weighted[:, j * LANES : (j + 1) * LANES]
        turned = jnp.dot(part, flip, preferred_element_type=jnp.float32).astype(jnp.bfloat16)
        for q in range(parts):
            for k in range(own_k):
                at = k * chans + q * share
                wall[me, q, k * share : (k + 1) * share, j * LANES : (j + 1) * LANES] = turned[at : at + share]

    pl.semaphore_wait(barrier, n - 1 + len(others))
    stage_peers()
    load_rec.wait()
    halo = pltpu.make_async_remote_copy(
        src_ref=rec_ref.at[:, pl.ds(0, length)], dst_ref=ext, send_sem=hsend, recv_sem=hrecv,
        device_id=(me, left), device_id_type=MESH,
    )
    halo.start()

    seed_row = lax.broadcasted_iota(jnp.int32, (SEED, LANES), 0)
    seed_col = lax.broadcasted_iota(jnp.int32, (SEED, LANES), 1)
    keep = seed_col + (SEED - 1) - seed_row < LANES

    def shifted(pieces, step):
        lane = lax.broadcasted_iota(jnp.int32, pieces[0].shape, 1)
        moved = [pltpu.roll(piece, LANES - step, 1) for piece in pieces]
        last = len(pieces) - 1
        return [jnp.where(lane < LANES - step, moved[m], moved[min(m + 1, last)]) for m in range(last + 1)]

    def frames_of(lines, s, count):
        turned = []
        for m in range(count):
            line = jnp.broadcast_to(lines[s : s + 1, m * LANES : (m + 1) * LANES], (SEED, LANES))
            turned.append(pltpu.roll(line, LANES - SEED + 1, 1, stride=1, stride_axis=0))
        block = [
            jnp.where(keep, turned[m], turned[min(m + 1, count - 1)]).astype(jnp.bfloat16)
            for m in range(count)
        ]
        step = SEED
        while step < LANES:
            ahead = shifted(block, step)
            block = [jnp.concatenate([ahead[m], block[m]], axis=0) for m in range(count)]
            step *= 2
        return block

    def build(start, first, last):
        lines = xf[pl.ds(start, 8), first * LANES : (last + 1) * LANES]
        for s in range(8):
            block = frames_of(lines, s, last + 1 - first)
            for m in range(first, last):
                g[start + s, :, m * LANES : (m + 1) * LANES] = block[m - first]

    def energies():
        total = [xf[:, m * LANES : (m + 1) * LANES] for m in range(chunks)]
        total = [piece * piece for piece in total]
        step = 1
        while step < LANES:
            total = [piece + later for piece, later in zip(total, shifted(total, step))]
            step *= 2
        energy = jnp.concatenate([sum(total[m + 1 : m + halves], total[m]) for m in range(own_blocks)], axis=1)
        scale[...] = lax.rsqrt(jnp.maximum(energy, 16.0))

    def own_part(index, carry):
        build(pl.multiple_of(index * 8, 8), 0, own_blocks - 1)
        return carry

    def rest(index, carry):
        start = pl.multiple_of(index * 8, 8)
        build(start, own_blocks - 1, chunks - 1)
        return carry

    def whole(index, carry):
        build(pl.multiple_of(index * 8, 8), 0, chunks - 1)
        return carry

    xf[:, :slab] = rec_ref[...].astype(jnp.float32)
    early = chans // 16
    lax.fori_loop(0, early, own_part, 0)
    halo.wait()
    borrowed = ext[...].astype(jnp.float32)
    xf[:, slab:] = jnp.where(tm == n_tm - 1, 0.0, borrowed)
    lax.fori_loop(0, early, rest, 0)
    stage_group()
    lax.fori_loop(early, chans // 8, whole, 0)
    stage_core()
    energies()

    size = own_k * share

    def widen(part):
        for i in range(n):
            start = pl.multiple_of((part * n + i) * size, size)
            for j in range(halves):
                wf[j, pl.ds(start, size), :] = wall[i, part, :, j * LANES : (j + 1) * LANES].astype(jnp.float32)

    def channels(part, index, acc):
        start = pl.multiple_of(part * share + index * 8, 8)
        scales = scale[pl.ds(start, 8), :]
        base = pl.multiple_of(part * n * size + index * 8, 8)
        for s in range(8):
            lhs = jnp.concatenate(
                [wf[j, pl.ds(base + s, n * own_k, stride=share), :] for j in range(halves)], axis=0
            ).astype(jnp.bfloat16)
            sums = jnp.dot(lhs, g[start + s], preferred_element_type=jnp.float32)
            total = sums[: n * own_k, :slab]
            for j in range(1, halves):
                total = total + sums[j * n * own_k : (j + 1) * n * own_k, j * LANES : j * LANES + slab]
            acc = acc + total * scales[s : s + 1, :]
        return acc

    def correlate(part, acc):
        widen(part)
        return lax.fori_loop(0, share // 8, functools.partial(channels, part), acc)

    acc = correlate(mine, jnp.zeros((n * own_k, slab), jnp.float32))
    if parts == 4:
        acc = correlate(theirs, acc)
    stage_end(0)
    acc = correlate(1 - core if parts == 2 else chip * 2 + 1 - core, acc)
    if parts == 4:
        stage_end(1)
        acc = correlate((1 - chip) * 2 + 1 - core, acc)
    for i in range(n):
        res[i] = acc[i * own_k : (i + 1) * own_k, :]

    results = []
    for d in range(1, n):
        peer = lax.rem(me + d, n)
        copy = pltpu.make_async_remote_copy(
            src_ref=res.at[peer], dst_ref=out_ref.at[me], send_sem=osend.at[d], recv_sem=orecv.at[d],
            device_id=(peer, tm), device_id_type=MESH,
        )
        copy.start()
        results.append(copy)
    out_ref[me] = res[me]
    for copy in sent:
        copy.wait_send()
    for d in range(1, n):
        results[d - 1].wait_send()
        source = lax.rem(me + n - d, n)
        pltpu.make_async_remote_copy(
            src_ref=res.at[source], dst_ref=out_ref.at[source], send_sem=osend.at[d], recv_sem=orecv.at[d],
            device_id=(source, tm), device_id_type=MESH,
        ).wait_recv()


def solution(mesh):
    n, n_tm = mesh.shape["tmpl"], mesh.shape["tm"]
    parts = 4

    def local(records, templates):
        _, chans, slab = records.shape
        own_k, _, length = templates.shape
        rows = own_k * chans
        return pl.pallas_call(
            functools.partial(kernel, n, n_tm, parts),
            out_shape=jax.ShapeDtypeStruct((n, own_k, slab), jnp.float32),
            in_specs=[pl.BlockSpec(memory_space=pl.ANY)] * 2,
            out_specs=pl.BlockSpec(memory_space=pltpu.VMEM),
            scratch_shapes=[
                pltpu.VMEM((chans, slab), jnp.bfloat16),
                pltpu.VMEM((rows, length), jnp.bfloat16),
                pltpu.VMEM((n, parts, rows // parts, length), jnp.bfloat16),
                pltpu.VMEM((length // LANES, n * rows, LANES), jnp.float32),
                pltpu.VMEM((chans, length), jnp.bfloat16),
                pltpu.VMEM((chans, slab + length), jnp.float32),
                pltpu.VMEM((chans, slab), jnp.float32),
                pltpu.VMEM((chans, LANES, slab + length - LANES), jnp.bfloat16),
                pltpu.VMEM((n, own_k, slab), jnp.float32),
                pltpu.SemaphoreType.DMA((2,)),
                pltpu.SemaphoreType.DMA,
                pltpu.SemaphoreType.DMA,
                pltpu.SemaphoreType.DMA((n,)),
                pltpu.SemaphoreType.DMA((n,)),
                pltpu.SemaphoreType.DMA((n,)),
                pltpu.SemaphoreType.DMA((n,)),
                pltpu.SemaphoreType.DMA((2 * n,)),
                pltpu.SemaphoreType.DMA((2 * n,)),
                pltpu.SemaphoreType.DMA((n,)),
                pltpu.SemaphoreType.DMA((n,)),
            ],
            compiler_params=pltpu.CompilerParams(
                collective_id=0, has_side_effects=True, vmem_limit_bytes=40 * 2**20
            ),
        )(records.reshape(chans, slab), templates.reshape(rows, length))

    placed = (P("tmpl", None, "tm"), P("tmpl", None, None))
    return jax.shard_map(
        local, mesh=mesh, in_specs=placed, out_specs=P(None, "tmpl", "tm"), check_vma=False
    )
```
